512 devices in a mesh: tok: 32 (over z, core), par: 16 (over x, y).
Axes of the slice: x: 4, y: 4, z: 16, core: 2. Of those that a mesh axis runs over, the one named last changes fastest.
Arguments:
- query_grads: bfloat16 [4, 8192, 28672], P(None, 'tok', 'par'), as said below
- start_block: bfloat16 [28672, 128], P('par', 'tok'), may hold values from -6 to 6
- hooked_out: bfloat16 [8192, 8192], P('tok', 'par'), may hold values from -6 to 6
- hooked_in: bfloat16 [8192, 28672], P('tok', 'par'), may hold values from -6 to 6
Outputs:
- scores: float32 [4, 8192], P(None, 'tok')
The draws below stay inside these ranges and needn't reach their ends.
Inputs may be any that keep to these rules, and one draw needn't show every extreme that they name: `query_grads`: Real-valued gradient matrices, of full rank.
All inputs are finite; a program needn't handle non-finite values.
Results may differ from the reference program's by a relative error of at most 0.006.
Values may be sent and summed in bfloat16 or wider, within the bound.
A program may use at most 64 MiB of HBM per device.

```python
import math
import jax
import jax.numpy as jnp
from jax import lax

DOUT = 8192
DIN = 28672
QUERIES = 4
RANK = 32
ITERS = 2
TOKENS = 8192


def draw_query_grads(key, part):
    key_base, key_rows, key_cols = jax.random.split(key, 3)
    base = jnp.clip(jax.random.normal(key_base, (QUERIES, DOUT, DIN), jnp.float32), -6.0, 6.0)
    row_scale = jnp.exp(jax.random.uniform(key_rows, (QUERIES, DOUT, 1), jnp.float32, 0.0, math.log(10.0)))
    col_scale = jnp.exp(jax.random.uniform(key_cols, (QUERIES, 1, DIN), jnp.float32, 0.0, math.log(10.0)))
    factor = 1.0 / (21.5 * math.sqrt(80.0 * DIN))
    return (base * row_scale * col_scale * factor).astype(jnp.bfloat16)


def block_levels(stream_key, shape, cuts, low, high):
    gain, own = 1.0, jax.random.fold_in(stream_key, 6)
    for dim, blocks in cuts:
        steps = jnp.exp(jax.random.uniform(jax.random.fold_in(own, dim), (blocks,), jnp.float32, low / len(cuts), high / len(cuts)))
        gain = gain * jnp.repeat(steps, shape[dim] // blocks).reshape([-1 if axis == dim else 1 for axis in range(len(shape))])
    return gain


def centred(key, shape, deviation, most, cuts=(), kind=jnp.bfloat16):
    level = block_levels(key, shape, cuts, -0.22, 0.18) if cuts else 1.0
    result = jax.random.normal(key, shape, jnp.float32) * deviation * level
    return jnp.minimum(jnp.maximum(result, -most), most).astype(kind)


def setup_inputs(seed: int = 0) -> dict:
    keys = jax.random.split(jax.random.key(seed), 5)
    query_grads = draw_query_grads(jax.random.fold_in(keys[4], 71), 0)
    start_block = centred(keys[1], (DIN, QUERIES * RANK), 1.0, 6.0, ((0, 16), (1, 32)))
    hooked_out = centred(keys[2], (TOKENS, DOUT), 1.0, 6.0, ((0, 32), (1, 16)))
    hooked_in = centred(keys[3], (TOKENS, DIN), 1.0, 6.0, ((0, 32), (1, 16)))
    return {"query_grads": query_grads, "start_block": start_block, "hooked_out": hooked_out, "hooked_in": hooked_in}


def local_gram(images):
    blocks = images.reshape(images.shape[0], QUERIES, RANK)
    return jnp.einsum('oqr,oqs->qrs', blocks, blocks, precision=lax.Precision.HIGHEST)

def from_gram(images, gram_sum):
    blocks = images.reshape(images.shape[0], QUERIES, RANK)
    chol_factor = jnp.linalg.cholesky(gram_sum)
    solved = lax.linalg.triangular_solve(chol_factor, jnp.transpose(blocks, (1, 2, 0)), left_side=True, lower=True)
    return jnp.transpose(solved, (2, 0, 1)).reshape(images.shape).astype(jnp.bfloat16)

def reference(query_grads, start_block, hooked_out, hooked_in):
    subspace = start_block
    full_basis = None
    for iteration in range(ITERS):
        pieces = []
        for query in range(QUERIES):
            cols = subspace[:, query * RANK:(query + 1) * RANK]
            pieces.append(jnp.dot(query_grads[query].astype(jnp.float32), cols.astype(jnp.float32), preferred_element_type=jnp.float32))
        images = jnp.concatenate(pieces, axis=1)
        full_basis = from_gram(images, local_gram(images))
        backs = []
        for query in range(QUERIES):
            cols = full_basis[:, query * RANK:(query + 1) * RANK]
            backs.append(jnp.dot(cols.T.astype(jnp.float32), query_grads[query].astype(jnp.float32), preferred_element_type=jnp.float32).T)
        subspace = jnp.concatenate(backs, axis=1).astype(jnp.bfloat16)
    out_proj = jnp.dot(hooked_out.astype(jnp.float32), full_basis.astype(jnp.float32), preferred_element_type=jnp.float32)
    in_proj = jnp.dot(hooked_in.astype(jnp.float32), subspace.astype(jnp.float32), preferred_element_type=jnp.float32)
    scores = (out_proj * in_proj).reshape(out_proj.shape[0], QUERIES, RANK).sum(axis=2)
    return scores.T
```

```python
import types

import jax
import jax.numpy as jnp
from jax import lax
from jax.experimental import pallas as pl
from jax.experimental.pallas import tpu as pltpu
from jax.sharding import PartitionSpec as P

MESH = pl.DeviceIdType.MESH
F32, BF16 = jnp.float32, jnp.bfloat16
HIGH = lax.Precision.HIGHEST
RANK = 32
ITERS = 2
QUERIES = 4
COLS = QUERIES * RANK
LANES = 128
Z = 16
PAR = 16
ROWS = 256
FEATS = 1792
TILES = FEATS // LANES
OUTS = 512
PIECE = 512
PIECES = 4
CHUNK = ROWS // PAR
HALF = COLS // 2

TREE = {0: (1, -1), 3: (1, -1), -3: (1, -1), 6: (1, -1, 2), -6: (1, -1)}
RELAYS = (6, -6, 3, -3)
ARRIVALS = (3, -3, 6, -6)
LEAVES = [(r, f) for r in (6, -6, 3, -3, 0) for f in TREE[r]]
ORDER = (10, 6, 9, 7, 11, 5, 2, 14, 8, 13, 3, 15, 1, 12, 4)


def nt(a, b, precision=None):
    return lax.dot_general(
        a, b, (((1,), (1,)), ((), ())), precision=precision, preferred_element_type=F32
    )


def remote(src, dst, send_sem, recv_sem, device):
    return pltpu.make_async_remote_copy(
        src_ref=src, dst_ref=dst, send_sem=send_sem, recv_sem=recv_sem,
        device_id=device, device_id_type=MESH,
    )


def drain(ref, sem):
    pltpu.make_async_copy(ref, ref, sem).wait()


def inverse_factor(gram):
    lane = lax.broadcasted_iota(jnp.int32, (RANK, COLS), 1)
    row = lax.broadcasted_iota(jnp.int32, (RANK, COLS), 0)
    first = lane - lane % RANK
    columns = [
        jnp.take_along_axis(gram, first + j, axis=1, mode="promise_in_bounds") for j in range(RANK)
    ]
    w = jnp.where(lane - first == row, 1.0, 0.0).astype(F32)
    for j in range(RANK):
        pivot = columns[j][j : j + 1, :]
        scale = lax.rsqrt(pivot)
        scale = scale * (1.5 - 0.5 * pivot * scale * scale)
        u = columns[j] * scale
        for k in range(j + 1, RANK):
            columns[k] = columns[k] - u * u[k : k + 1, :]
        row_w = w[j : j + 1, :] * scale
        w = jnp.where(row == j, row_w, jnp.where(row > j, w - u * row_w, w))
    return w


def block_diagonal(w):
    rows = lax.broadcasted_iota(jnp.int32, (COLS, COLS), 0)
    lanes = lax.broadcasted_iota(jnp.int32, (COLS, COLS), 1)
    return jnp.where(rows // RANK == lanes // RANK, jnp.concatenate([w] * QUERIES, axis=0), 0.0)


def kernel(names, *refs):
    m = types.SimpleNamespace(**dict(zip(names, refs)))
    tok, par = lax.axis_index("tok"), lax.axis_index("par")
    z, core = tok // 2, tok % 2

    def chip(offset):
        return (lax.rem(tok + 2 * offset + 2 * Z, 2 * Z), par)

    def at_z(offset):
        return lax.rem(z + offset + Z, Z)

    def peer(k):
        return lax.rem(par + k, PAR)

    sent = []
    sibling = (tok + 1 - 2 * core, par)

    loads = [
        pltpu.make_async_copy(m.grads.at[q], m.g.at[q], m.load_sem.at[q])
        for q in range(QUERIES)
    ] + [
        pltpu.make_async_copy(m.hook_out, m.ho, m.load_sem.at[QUERIES]),
        pltpu.make_async_copy(m.hook_in, m.hi, m.load_sem.at[QUERIES + 1]),
    ]
    barrier = pltpu.get_barrier_semaphore()
    for k in range(1, Z):
        pl.semaphore_signal(barrier, inc=1, device_id=chip(k), device_id_type=MESH)
    pl.semaphore_signal(barrier, inc=1, device_id=sibling, device_id_type=MESH)
    for k in range(1, PAR):
        pl.semaphore_signal(barrier, inc=1, device_id=(tok, peer(k)), device_id_type=MESH)

    for load in loads:
        load.start()

    start = m.start[...].astype(F32)
    tail = jnp.concatenate(
        [start[:, 3 * PIECE :], jnp.zeros((start.shape[0], PIECES * PIECE - FEATS), F32)], axis=1
    )
    pieces = [start[:, k * PIECE : (k + 1) * PIECE] for k in range(PIECES - 1)] + [tail]
    m.s0[core, z] = jnp.concatenate(pieces, axis=0).astype(BF16)
    for it in range(ITERS):
        for k in range(TILES, Z):
            m.part[it, k] = jnp.zeros((HALF, LANES), F32)

    pl.semaphore_wait(barrier, Z - 1 + 1 + PAR - 1)

    def z_gather(buf, send_sem, recv_sem):
        own = buf.at[z]
        for r in RELAYS + TREE[0]:
            remote(own, own, send_sem, recv_sem.at[r % Z], chip(r)).start()
        for r in ARRIVALS:
            block = buf.at[at_z(-r)]
            drain(block, recv_sem.at[r % Z])
            for f in TREE[r]:
                remote(block, block, send_sem, recv_sem.at[(r + f) % Z], chip(f)).start()
        relayed = [r % Z for r in RELAYS]
        for k in range(1, Z):
            if k not in relayed:
                drain(buf.at[at_z(-k)], recv_sem.at[k])
        sent.append((buf.at[pl.ds(0, Z - 1)], send_sem))

    def par_scatter(src, dst, send_sem, recv_sem):
        for k in ORDER:
            remote(src.at[peer(k)], dst.at[k - 1], send_sem, recv_sem, (tok, peer(k))).start()
        sent.append((dst, send_sem))

    def par_gather(buf, send_sem, recv_sem):
        own = buf.at[par]
        for k in ORDER:
            remote(own, own, send_sem, recv_sem, (tok, peer(k))).start()
        sent.append((buf.at[pl.ds(0, PAR - 1)], send_sem))

    def swap(buf, send_sem, recv_sem):
        remote(buf.at[core], buf.at[core], send_sem, recv_sem, sibling).start()
        sent.append((buf.at[core], send_sem))

    z_gather(m.s0.at[core], m.s0_ss.at[0], m.s0_rs)
    swap(m.s0, m.s0_ss.at[1], m.s0_rs.at[0])
    for q in range(QUERIES):
        loads[q].wait()
    drain(m.s0.at[1 - core], m.s0_rs.at[0])
    even, odd = m.s0[0].astype(F32), m.s0[1].astype(F32)
    for k in range(PIECES):
        rows = slice(k * 4, k * 4 + 4)
        both = jnp.concatenate([even[:, rows, :], odd[:, rows, :]], axis=1)
        m.s0t[:, k * PIECE : (k + 1) * PIECE] = both.reshape(COLS, PIECE).astype(BF16)
    images = jnp.concatenate(
        [nt(m.g[q], m.s0t[q * RANK : (q + 1) * RANK, :FEATS]) for q in range(QUERIES)], axis=1
    )

    def tiles_of(buf, plane, first):
        return jnp.concatenate(
            [buf[plane, k, first : first + RANK, :] for k in range(TILES)], axis=1
        )

    for it in range(ITERS):
        m.img[it] = images.reshape(PAR, CHUNK, COLS)
        par_scatter(m.img.at[it], m.img_in.at[it], m.img_ss.at[it], m.img_rs.at[it])
        drain(m.img_in.at[it], m.img_rs.at[it])
        m.whole[it, par] = m.img[it, par] + jnp.sum(m.img_in[it], axis=0)
        par_gather(m.whole.at[it], m.whole_ss.at[it], m.whole_rs.at[it])
        drain(m.whole.at[it, pl.ds(0, PAR - 1)], m.whole_rs.at[it])

        if it == ITERS - 1:
            @pl.when(z == par)
            def _():
                for k in range(1, Z):
                    remote(
                        m.whole.at[it, at_z(k)], m.brow, m.brow_ss, m.brow_rs, chip(k)
                    ).start()
                m.brow_own[...] = m.whole[it, z]

        turned = m.whole[it].reshape(ROWS, COLS).T
        gram = nt(turned, turned, HIGH)
        lane = lax.broadcasted_iota(jnp.int32, (RANK, COLS), 1)
        packed = jnp.zeros((RANK, COLS), F32)
        for q in range(QUERIES):
            packed = jnp.where(lane // RANK == q, gram[q * RANK : (q + 1) * RANK, :], packed)
        m.gram_out[it] = packed
        remote(
            m.gram_out.at[it], m.gram_in.at[it],
            m.gram_ss.at[it, 0], m.gram_rs.at[it, 0], sibling,
        ).start()
        sent.append((m.gram_out.at[it], m.gram_ss.at[it, 0]))

        high = turned.astype(BF16)
        low = (turned - high.astype(F32)).astype(BF16)
        for q in range(QUERIES):
            cut = slice(q * RANK, (q + 1) * RANK)
            m.split[q] = jnp.concatenate([high[cut], low[cut]], axis=0)

        def back(q):
            both = jnp.dot(m.split[q], m.g[q], preferred_element_type=F32)
            return both[:RANK] + both[RANK:]

        for i in range(2):
            terms = back(2 * (1 - core) + i)
            for k in range(TILES):
                m.give[it, i, k] = terms[:, k * LANES : (k + 1) * LANES]
            remote(
                m.give.at[it, i], m.take.at[it, i],
                m.give_ss.at[it, i], m.take_rs.at[it, i], sibling,
            ).start()
            sent.append((m.give.at[it, i], m.give_ss.at[it, i]))

        drain(m.gram_in.at[it], m.gram_rs.at[it, 0])
        m.gram_rows[it] = (packed + m.gram_in[it]).reshape(PAR, 2, COLS)
        mine = m.gram_rows.at[it, par]
        for k in range(1, Z):
            remote(
                mine, m.gram_z.at[it, k - 1], m.gram_ss.at[it, 1], m.gram_rs.at[it, 1], chip(k)
            ).start()
        sent.append((m.gram_z.at[it], m.gram_ss.at[it, 1]))

        for i in range(2):
            terms = back(2 * core + i)
            drain(m.take.at[it, i], m.take_rs.at[it, i])
            for k in range(TILES):
                both = terms[:, k * LANES : (k + 1) * LANES] + m.take[it, i, k]
                m.part[it, k, i * RANK : (i + 1) * RANK, :] = both

        part = m.part.at[it]
        for slot, (r, f) in enumerate(LEAVES):
            remote(
                part.at[at_z(-r - f)], m.leaf.at[it, slot],
                m.leaf_ss.at[it], m.leaf_rs.at[it, slot], chip(-f),
            ).start()
        sent.append((m.leaf.at[it], m.leaf_ss.at[it]))

        drain(m.gram_z.at[it], m.gram_rs.at[it, 1])
        m.gram_all[it, par] = m.gram_rows[it, par] + jnp.sum(m.gram_z[it], axis=0)
        par_gather(m.gram_all.at[it], m.gram_ss.at[it, 2], m.gram_rs.at[it, 2])

        for n, r in enumerate(RELAYS):
            total = m.part[it, at_z(-r)]
            for slot, (rr, f) in enumerate(LEAVES):
                if rr == r:
                    drain(m.leaf.at[it, slot], m.leaf_rs.at[it, slot])
                    total = total + m.leaf[it, slot]
            m.relay[it, n] = total.astype(BF16)
            remote(
                m.relay.at[it, n], m.final.at[it, n],
                m.relay_ss.at[it], m.final_rs.at[it, n], chip(-r),
            ).start()
        sent.append((m.relay.at[it], m.relay_ss.at[it]))

        drain(m.gram_all.at[it, pl.ds(0, PAR - 1)], m.gram_rs.at[it, 2])
        full = m.gram_all[it].reshape(RANK, COLS)
        inverse = block_diagonal(inverse_factor(full))
        inverse_mine = jnp.where(
            core == 0, inverse[:HALF, :HALF], inverse[HALF:, HALF:]
        )

        total = m.part[it, z]
        for slot, (r, f) in enumerate(LEAVES):
            if r == 0:
                drain(m.leaf.at[it, slot], m.leaf_rs.at[it, slot])
                total = total + m.leaf[it, slot]
        for n in range(len(RELAYS)):
            drain(m.final.at[it, n], m.final_rs.at[it, n])
            total = total + m.final[it, n].astype(F32)
        turned_back = jnp.dot(inverse_mine, total, precision=HIGH, preferred_element_type=F32)
        sub = m.sub if it < ITERS - 1 else m.last
        sub[core, z, :HALF, :] = turned_back.astype(BF16)
        if it == ITERS - 1:
            @pl.when(z != par)
            def _():
                drain(m.brow, m.brow_rs)
                m.brow_own[...] = m.brow[...]
            sub[core, z, HALF:, :] = nt(m.brow_own[...], inverse, HIGH).astype(BF16)

        z_gather(sub.at[core], m.sub_ss.at[it, 0], m.sub_rs.at[it])
        swap(sub, m.sub_ss.at[it, 1], m.sub_rs.at[it, 0])
        if it < ITERS - 1:
            def pair(plane):
                return jnp.concatenate(
                    [nt(m.g[2 * plane + i], tiles_of(sub, plane, i * RANK)) for i in range(2)], axis=1
                )

            ours = pair(core)
            drain(sub.at[1 - core], m.sub_rs.at[it, 0])
            theirs = pair(1 - core)
            images = jnp.where(
                core == 0,
                jnp.concatenate([ours, theirs], axis=1),
                jnp.concatenate([theirs, ours], axis=1),
            )
        else:
            drain(sub.at[1 - core], m.sub_rs.at[it, 0])

    loads[QUERIES].wait()
    loads[QUERIES + 1].wait()
    last = m.last
    basis = jnp.concatenate(
        [last[plane, :, HALF:, :].reshape(ROWS, COLS) for plane in range(2)], axis=0
    )
    out_proj = jnp.dot(m.ho[...], basis, preferred_element_type=F32)
    subspace = jnp.concatenate(
        [tiles_of(last, q // 2, (q % 2) * RANK) for q in range(QUERIES)], axis=0
    )
    in_proj = nt(m.hi[...], subspace)
    m.proj[:, :CHUNK, :] = out_proj.reshape(PAR, CHUNK, COLS)
    m.proj[:, CHUNK:, :] = in_proj.reshape(PAR, CHUNK, COLS)
    par_scatter(m.proj, m.proj_in, m.proj_ss, m.proj_rs)
    lane8 = lax.broadcasted_iota(jnp.int32, (8, COLS), 1)
    row8 = lax.broadcasted_iota(jnp.int32, (8, COLS), 0)
    pick = jnp.where(lane8 // RANK == row8, 1.0, 0.0).astype(F32)
    m.placed[...] = jnp.zeros((LANES, COLS), F32)
    drain(m.proj_in, m.proj_rs)
    total = m.proj[par] + jnp.sum(m.proj_in[...], axis=0)
    m.placed[pl.ds(pl.multiple_of((par % 8) * CHUNK, CHUNK), CHUNK), :] = (
        total[:CHUNK] * total[CHUNK:]
    )
    m.score[par] = nt(pick, m.placed[...], HIGH)
    par_gather(m.score, m.score_ss, m.score_rs)
    drain(m.score.at[pl.ds(0, PAR - 1)], m.score_rs)
    for h in range(2):
        m.out[:, h * LANES : (h + 1) * LANES] = jnp.sum(
            m.score[h * 8 : h * 8 + 8], axis=0
        )[:QUERIES]

    for ref, sem in sent:
        drain(ref, sem)

    @pl.when(z == par)
    def _():
        drain(m.whole.at[ITERS - 1, pl.ds(0, Z - 1)], m.brow_ss)


def on_device(query_grads, start_block, hooked_out, hooked_in):
    vmem, dma = pltpu.VMEM, pltpu.SemaphoreType.DMA
    scratch = dict(
        g=vmem((QUERIES, ROWS, FEATS), BF16),
        ho=vmem((ROWS, OUTS), BF16),
        hi=vmem((ROWS, FEATS), BF16),
        load_sem=dma((QUERIES + 2,)),
        s0=vmem((2, Z, 4 * PIECES, PIECE), BF16),
        s0_ss=dma((2,)),
        s0_rs=dma((Z,)),
        s0t=vmem((COLS, PIECES * PIECE), BF16),
        img=vmem((ITERS, PAR, CHUNK, COLS), F32),
        img_in=vmem((ITERS, PAR - 1, CHUNK, COLS), F32),
        img_ss=dma((ITERS,)),
        img_rs=dma((ITERS,)),
        whole=vmem((ITERS, PAR, CHUNK, COLS), F32),
        whole_ss=dma((ITERS,)),
        whole_rs=dma((ITERS,)),
        brow=vmem((CHUNK, COLS), F32),
        brow_own=vmem((CHUNK, COLS), F32),
        brow_ss=dma,
        brow_rs=dma,
        gram_out=vmem((ITERS, RANK, COLS), F32),
        gram_in=vmem((ITERS, RANK, COLS), F32),
        gram_rows=vmem((ITERS, PAR, 2, COLS), F32),
        gram_z=vmem((ITERS, Z - 1, 2, COLS), F32),
        gram_all=vmem((ITERS, PAR, 2, COLS), F32),
        gram_ss=dma((ITERS, 3)),
        gram_rs=dma((ITERS, 3)),
        split=vmem((QUERIES, 2 * RANK, ROWS), BF16),
        give=vmem((ITERS, 2, TILES, RANK, LANES), F32),
        take=vmem((ITERS, 2, TILES, RANK, LANES), F32),
        give_ss=dma((ITERS, 2)),
        take_rs=dma((ITERS, 2)),
        part=vmem((ITERS, Z, HALF, LANES), F32),
        leaf=vmem((ITERS, len(LEAVES), HALF, LANES), F32),
        leaf_ss=dma((ITERS,)),
        leaf_rs=dma((ITERS, len(LEAVES))),
        relay=vmem((ITERS, len(RELAYS), HALF, LANES), BF16),
        final=vmem((ITERS, len(RELAYS), HALF, LANES), BF16),
        relay_ss=dma((ITERS,)),
        final_rs=dma((ITERS, len(RELAYS))),
        sub=vmem((2, Z, HALF, LANES), BF16),
        last=vmem((2, Z, HALF + CHUNK, LANES), BF16),
        sub_ss=dma((ITERS, 2)),
        sub_rs=dma((ITERS, Z)),
        proj=vmem((PAR, 2 * CHUNK, COLS), F32),
        proj_in=vmem((PAR - 1, 2 * CHUNK, COLS), F32),
        proj_ss=dma,
        proj_rs=dma,
        placed=vmem((LANES, COLS), F32),
        score=vmem((PAR, 8, LANES), F32),
        score_ss=dma,
        score_rs=dma,
    )
    names = ["grads", "start", "hook_out", "hook_in", "out"] + list(scratch)
    hbm = pl.BlockSpec(memory_space=pltpu.HBM)
    near = pl.BlockSpec(memory_space=pltpu.VMEM)

    def body(*refs):
        kernel(names, *refs)

    return pl.pallas_call(
        body,
        name="influence",
        out_shape=jax.ShapeDtypeStruct((QUERIES, ROWS), F32),
        in_specs=[hbm, near, hbm, hbm],
        out_specs=near,
        scratch_shapes=list(scratch.values()),
        compiler_params=pltpu.CompilerParams(
            collective_id=0, has_side_effects=True, vmem_limit_bytes=60 * 1024 * 1024
        ),
        cost_estimate=pl.CostEstimate(
            flops=8 * QUERIES * ROWS * FEATS * RANK, bytes_accessed=5_000_000, transcendentals=0
        ),
    )(query_grads, start_block.T, hooked_out, hooked_in)


def solution(mesh):
    placed = (P(None, "tok", "par"), P("par", "tok"), P("tok", "par"), P("tok", "par"))
    return jax.shard_map(
        on_device, mesh=mesh, in_specs=placed, out_specs=P(None, "tok"), check_vma=False
    )
```

```python
import types

import jax
import jax.numpy as jnp
from jax import lax
from jax.experimental import pallas as pl
from jax.experimental.pallas import tpu as pltpu
from jax.sharding import PartitionSpec as P

MESH = pl.DeviceIdType.MESH
F32, BF16 = jnp.float32, jnp.bfloat16
HIGH = lax.Precision.HIGHEST
RANK = 32
ITERS = 2
QUERIES = 4
COLS = QUERIES * RANK
LANES = 128
Z = 16
PAR = 16
ROWS = 256
FEATS = 1792
TILES = FEATS // LANES
OUTS = 512
PIECE = 512
PIECES = 4
CHUNK = ROWS // PAR
HALF = COLS // 2

TREE = {0: (1, -1), 3: (1, -1), -3: (1, -1), 6: (1, -1, 2), -6: (1, -1)}
RELAYS = (6, -6, 3, -3)
FAR = (8, 7, 9, 6, 10, 5, 11, 4, 12, 3, 13, 2, 14, 1, 15)
FAN = {0: (1, -1, 2, -2), 5: (1, -1, 2, -2, 3), -5: (1, -1, 2, -2)}
LEAVES = [(r, f) for r in (6, -6, 3, -3, 0) for f in TREE[r]]
SIDE = 4
ORDER = (10, 6, 14, 9, 11, 2, 8, 5, 15, 7, 13, 1, 3, 4, 12)


def nt(a, b, precision=None):
    return lax.dot_general(
        a, b, (((1,), (1,)), ((), ())), precision=precision, preferred_element_type=F32
    )


def remote(src, dst, send_sem, recv_sem, device):
    return pltpu.make_async_remote_copy(
        src_ref=src, dst_ref=dst, send_sem=send_sem, recv_sem=recv_sem,
        device_id=device, device_id_type=MESH,
    )


def drain(ref, sem):
    pltpu.make_async_copy(ref, ref, sem).wait()


def inverse_factor(gram):
    lane = lax.broadcasted_iota(jnp.int32, (RANK, COLS), 1)
    row = lax.broadcasted_iota(jnp.int32, (RANK, COLS), 0)
    first = lane - lane % RANK
    columns = [
        jnp.take_along_axis(gram, first + j, axis=1, mode="promise_in_bounds") for j in range(RANK)
    ]
    w = jnp.where(lane - first == row, 1.0, 0.0).astype(F32)
    for j in range(RANK):
        pivot = columns[j][j : j + 1, :]
        scale = lax.rsqrt(pivot)
        scale = scale * (1.5 - 0.5 * pivot * scale * scale)
        u = columns[j] * scale
        for k in range(j + 1, RANK):
            columns[k] = columns[k] - u * u[k : k + 1, :]
        row_w = w[j : j + 1, :] * scale
        w = jnp.where(row == j, row_w, jnp.where(row > j, w - u * row_w, w))
    return w


def block_diagonal(w):
    rows = lax.broadcasted_iota(jnp.int32, (COLS, COLS), 0)
    lanes = lax.broadcasted_iota(jnp.int32, (COLS, COLS), 1)
    return jnp.where(rows // RANK == lanes // RANK, jnp.concatenate([w] * QUERIES, axis=0), 0.0)


def kernel(names, *refs):
    m = types.SimpleNamespace(**dict(zip(names, refs)))
    tok, par = lax.axis_index("tok"), lax.axis_index("par")
    z, core = tok // 2, tok % 2

    def chip(offset):
        return (lax.rem(tok + 2 * offset + 2 * Z, 2 * Z), par)

    def at_z(offset):
        return lax.rem(z + offset + Z, Z)

    def peer(k):
        return lax.rem(par // SIDE + k // SIDE, SIDE) * SIDE + lax.rem(par + k, SIDE)

    sent = []
    sibling = (tok + 1 - 2 * core, par)

    loads = [
        pltpu.make_async_copy(m.grads.at[q], m.g.at[q], m.load_sem.at[q])
        for q in range(QUERIES)
    ] + [
        pltpu.make_async_copy(m.hook_out, m.ho, m.load_sem.at[QUERIES]),
        pltpu.make_async_copy(m.hook_in, m.hi, m.load_sem.at[QUERIES + 1]),
    ]
    load_start = pltpu.make_async_copy(m.start, m.begin, m.load_sem.at[QUERIES + 2])
    load_start.start()
    barrier = pltpu.get_barrier_semaphore()
    for k in FAR:
        pl.semaphore_signal(barrier, inc=1, device_id=chip(k), device_id_type=MESH)
    pl.semaphore_signal(barrier, inc=1, device_id=sibling, device_id_type=MESH)
    for k in ORDER:
        pl.semaphore_signal(barrier, inc=1, device_id=(tok, peer(k)), device_id_type=MESH)

    for load in loads:
        load.start()

    load_start.wait()
    start = m.begin[...].astype(F32)
    tail = jnp.concatenate(
        [start[:, 3 * PIECE :], jnp.zeros((start.shape[0], PIECES * PIECE - FEATS), F32)], axis=1
    )
    pieces = [start[:, k * PIECE : (k + 1) * PIECE] for k in range(PIECES - 1)] + [tail]
    m.s0[core, z] = jnp.concatenate(pieces, axis=0).astype(BF16)
    for it in range(ITERS):
        for k in range(TILES, Z):
            m.part[it, k] = jnp.zeros((HALF, LANES), F32)

    pl.semaphore_wait(barrier, Z - 1 + 1 + PAR - 1)

    def z_gather(buf, send_sem, recv_sem):
        own = buf.at[z]
        for r in (5, -5) + FAN[0]:
            remote(own, own, send_sem, recv_sem.at[r % Z], chip(r)).start()
        for r in (5, -5):
            block = buf.at[at_z(-r)]
            drain(block, recv_sem.at[r % Z])
            for f in FAN[r]:
                remote(block, block, send_sem, recv_sem.at[(r + f) % Z], chip(f)).start()
        relayed = [r % Z for r in (5, -5)]
        for k in range(1, Z):
            if k not in relayed:
                drain(buf.at[at_z(-k)], recv_sem.at[k])
        sent.append((buf.at[pl.ds(0, Z - 1)], send_sem))

    def par_scatter(src, dst, send_sem, recv_sem):
        for k in ORDER:
            remote(src.at[peer(k)], dst.at[k - 1], send_sem, recv_sem, (tok, peer(k))).start()
        sent.append((dst, send_sem))

    def par_gather(buf, send_sem, recv_sem):
        own = buf.at[par]
        for k in ORDER:
            remote(own, own, send_sem, recv_sem, (tok, peer(k))).start()
        sent.append((buf.at[pl.ds(0, PAR - 1)], send_sem))

    def swap(buf, send_sem, recv_sem):
        remote(buf.at[core], buf.at[core], send_sem, recv_sem, sibling).start()
        sent.append((buf.at[core], send_sem))

    z_gather(m.s0.at[core], m.s0_ss.at[0], m.s0_rs)
    swap(m.s0, m.s0_ss.at[1], m.s0_rs.at[0])
    for q in range(QUERIES):
        loads[q].wait()
    drain(m.s0.at[1 - core], m.s0_rs.at[0])
    even, odd = m.s0[0].astype(F32), m.s0[1].astype(F32)
    for k in range(PIECES):
        rows = slice(k * 4, k * 4 + 4)
        both = jnp.concatenate([even[:, rows, :], odd[:, rows, :]], axis=1)
        m.s0t[:, k * PIECE : (k + 1) * PIECE] = both.reshape(COLS, PIECE).astype(BF16)
    images = jnp.concatenate(
        [nt(m.g[q], m.s0t[q * RANK : (q + 1) * RANK, :FEATS]) for q in range(QUERIES)], axis=1
    )

    def tiles_of(buf, plane, first):
        return jnp.concatenate(
            [buf[plane, k, first : first + RANK, :] for k in range(TILES)], axis=1
        )

    for it in range(ITERS):
        m.img[it] = images.reshape(PAR, CHUNK, COLS)
        par_scatter(m.img.at[it], m.img_in.at[it], m.img_ss.at[it], m.img_rs.at[it])
        drain(m.img_in.at[it], m.img_rs.at[it])
        m.whole[it, par] = m.img[it, par] + jnp.sum(m.img_in[it], axis=0)
        par_gather(m.whole.at[it], m.whole_ss.at[it], m.whole_rs.at[it])
        drain(m.whole.at[it, pl.ds(0, PAR - 1)], m.whole_rs.at[it])

        if it == ITERS - 1:
            @pl.when(z == par)
            def _():
                for k in FAR:
                    remote(
                        m.whole.at[it, at_z(k)], m.brow, m.brow_ss, m.brow_rs, chip(k)
                    ).start()
                m.brow_own[...] = m.whole[it, z]

        turned = m.whole[it].reshape(ROWS, COLS).T
        gram = nt(turned, turned, HIGH)
        lane = lax.broadcasted_iota(jnp.int32, (RANK, COLS), 1)
        packed = jnp.zeros((RANK, COLS), F32)
        for q in range(QUERIES):
            packed = jnp.where(lane // RANK == q, gram[q * RANK : (q + 1) * RANK, :], packed)
        m.gram_out[it] = packed
        remote(
            m.gram_out.at[it], m.gram_in.at[it],
            m.gram_ss.at[it, 0], m.gram_rs.at[it, 0], sibling,
        ).start()
        sent.append((m.gram_out.at[it], m.gram_ss.at[it, 0]))

        high = turned.astype(BF16)
        low = (turned - high.astype(F32)).astype(BF16)
        for q in range(QUERIES):
            cut = slice(q * RANK, (q + 1) * RANK)
            m.split[q] = jnp.concatenate([high[cut], low[cut]], axis=0)

        def back(q):
            both = jnp.dot(m.split[q], m.g[q], preferred_element_type=F32)
            return both[:RANK] + both[RANK:]

        for i in range(2):
            terms = back(2 * (1 - core) + i)
            for k in range(TILES):
                m.give[it, i, k] = terms[:, k * LANES : (k + 1) * LANES]
            remote(
                m.give.at[it, i], m.take.at[it, i],
                m.give_ss.at[it, i], m.take_rs.at[it, i], sibling,
            ).start()
            sent.append((m.give.at[it, i], m.give_ss.at[it, i]))

        drain(m.gram_in.at[it], m.gram_rs.at[it, 0])
        m.gram_rows[it] = (packed + m.gram_in[it]).reshape(PAR, 2, COLS)
        mine = m.gram_rows.at[it, par]
        for k in FAR:
            remote(
                mine, m.gram_z.at[it, k - 1], m.gram_ss.at[it, 1], m.gram_rs.at[it, 1], chip(k)
            ).start()
        sent.append((m.gram_z.at[it], m.gram_ss.at[it, 1]))

        for i in range(2):
            terms = back(2 * core + i)
            drain(m.take.at[it, i], m.take_rs.at[it, i])
            for k in range(TILES):
                both = terms[:, k * LANES : (k + 1) * LANES] + m.take[it, i, k]
                m.part[it, k, i * RANK : (i + 1) * RANK, :] = both

        part = m.part.at[it]
        for slot, (r, f) in enumerate(LEAVES):
            remote(
                part.at[at_z(-r - f)], m.leaf.at[it, slot],
                m.leaf_ss.at[it], m.leaf_rs.at[it, slot], chip(-f),
            ).start()
        sent.append((m.leaf.at[it], m.leaf_ss.at[it]))

        drain(m.gram_z.at[it], m.gram_rs.at[it, 1])
        m.gram_all[it, par] = m.gram_rows[it, par] + jnp.sum(m.gram_z[it], axis=0)
        par_gather(m.gram_all.at[it], m.gram_ss.at[it, 2], m.gram_rs.at[it, 2])

        for n, r in enumerate(RELAYS):
            total = m.part[it, at_z(-r)]
            for slot, (rr, f) in enumerate(LEAVES):
                if rr == r:
                    drain(m.leaf.at[it, slot], m.leaf_rs.at[it, slot])
                    total = total + m.leaf[it, slot]
            m.relay[it, n] = total.astype(BF16)
            remote(
                m.relay.at[it, n], m.final.at[it, n],
                m.relay_ss.at[it], m.final_rs.at[it, n], chip(-r),
            ).start()
        sent.append((m.relay.at[it], m.relay_ss.at[it]))

        drain(m.gram_all.at[it, pl.ds(0, PAR - 1)], m.gram_rs.at[it, 2])
        full = m.gram_all[it].reshape(RANK, COLS)
        inverse = block_diagonal(inverse_factor(full))
        inverse_mine = jnp.where(
            core == 0, inverse[:HALF, :HALF], inverse[HALF:, HALF:]
        )

        total = m.part[it, z]
        for slot, (r, f) in enumerate(LEAVES):
            if r == 0:
                drain(m.leaf.at[it, slot], m.leaf_rs.at[it, slot])
                total = total + m.leaf[it, slot]
        for n in range(len(RELAYS)):
            drain(m.final.at[it, n], m.final_rs.at[it, n])
            total = total + m.final[it, n].astype(F32)
        turned_back = jnp.dot(inverse_mine, total, precision=HIGH, preferred_element_type=F32)
        sub = m.sub if it < ITERS - 1 else m.last
        sub[core, z, :HALF, :] = turned_back.astype(BF16)
        if it == ITERS - 1:
            @pl.when(z != par)
            def _():
                drain(m.brow, m.brow_rs)
                m.brow_own[...] = m.brow[...]
            sub[core, z, HALF:, :] = nt(m.brow_own[...], inverse, HIGH).astype(BF16)

        z_gather(sub.at[core], m.sub_ss.at[it, 0], m.sub_rs.at[it])
        swap(sub, m.sub_ss.at[it, 1], m.sub_rs.at[it, 0])
        if it < ITERS - 1:
            def pair(plane):
                return jnp.concatenate(
                    [nt(m.g[2 * plane + i], tiles_of(sub, plane, i * RANK)) for i in range(2)], axis=1
                )

            ours = pair(core)
            drain(sub.at[1 - core], m.sub_rs.at[it, 0])
            theirs = pair(1 - core)
            images = jnp.where(
                core == 0,
                jnp.concatenate([ours, theirs], axis=1),
                jnp.concatenate([theirs, ours], axis=1),
            )
        else:
            drain(sub.at[1 - core], m.sub_rs.at[it, 0])

    loads[QUERIES].wait()
    loads[QUERIES + 1].wait()
    last = m.last
    basis = jnp.concatenate(
        [last[plane, :, HALF:, :].reshape(ROWS, COLS) for plane in range(2)], axis=0
    )
    out_proj = jnp.dot(m.ho[...], basis, preferred_element_type=F32)
    subspace = jnp.concatenate(
        [tiles_of(last, q // 2, (q % 2) * RANK) for q in range(QUERIES)], axis=0
    )
    in_proj = nt(m.hi[...], subspace)
    m.proj[:, :CHUNK, :] = out_proj.reshape(PAR, CHUNK, COLS)
    m.proj[:, CHUNK:, :] = in_proj.reshape(PAR, CHUNK, COLS)
    par_scatter(m.proj, m.proj_in, m.proj_ss, m.proj_rs)
    lane8 = lax.broadcasted_iota(jnp.int32, (8, COLS), 1)
    row8 = lax.broadcasted_iota(jnp.int32, (8, COLS), 0)
    pick = jnp.where(lane8 // RANK == row8, 1.0, 0.0).astype(F32)
    m.placed[...] = jnp.zeros((LANES, COLS), F32)
    drain(m.proj_in, m.proj_rs)
    total = m.proj[par] + jnp.sum(m.proj_in[...], axis=0)
    m.placed[pl.ds(pl.multiple_of((par % 8) * CHUNK, CHUNK), CHUNK), :] = (
        total[:CHUNK] * total[CHUNK:]
    )
    m.score[par] = nt(pick, m.placed[...], HIGH)
    par_gather(m.score, m.score_ss, m.score_rs)
    drain(m.score.at[pl.ds(0, PAR - 1)], m.score_rs)
    for h in range(2):
        m.out[:, h * LANES : (h + 1) * LANES] = jnp.sum(
            m.score[h * 8 : h * 8 + 8], axis=0
        )[:QUERIES]

    for ref, sem in sent:
        drain(ref, sem)

    @pl.when(z == par)
    def _():
        drain(m.whole.at[ITERS - 1, pl.ds(0, Z - 1)], m.brow_ss)


def on_device(query_grads, start_block, hooked_out, hooked_in):
    vmem, dma = pltpu.VMEM, pltpu.SemaphoreType.DMA
    scratch = dict(
        g=vmem((QUERIES, ROWS, FEATS), BF16),
        ho=vmem((ROWS, OUTS), BF16),
        hi=vmem((ROWS, FEATS), BF16),
        begin=vmem((QUERIES, FEATS), BF16),
        load_sem=dma((QUERIES + 3,)),
        s0=vmem((2, Z, 4 * PIECES, PIECE), BF16),
        s0_ss=dma((2,)),
        s0_rs=dma((Z,)),
        s0t=vmem((COLS, PIECES * PIECE), BF16),
        img=vmem((ITERS, PAR, CHUNK, COLS), F32),
        img_in=vmem((ITERS, PAR - 1, CHUNK, COLS), F32),
        img_ss=dma((ITERS,)),
        img_rs=dma((ITERS,)),
        whole=vmem((ITERS, PAR, CHUNK, COLS), F32),
        whole_ss=dma((ITERS,)),
        whole_rs=dma((ITERS,)),
        brow=vmem((CHUNK, COLS), F32),
        brow_own=vmem((CHUNK, COLS), F32),
        brow_ss=dma,
        brow_rs=dma,
        gram_out=vmem((ITERS, RANK, COLS), F32),
        gram_in=vmem((ITERS, RANK, COLS), F32),
        gram_rows=vmem((ITERS, PAR, 2, COLS), F32),
        gram_z=vmem((ITERS, Z - 1, 2, COLS), F32),
        gram_all=vmem((ITERS, PAR, 2, COLS), F32),
        gram_ss=dma((ITERS, 3)),
        gram_rs=dma((ITERS, 3)),
        split=vmem((QUERIES, 2 * RANK, ROWS), BF16),
        give=vmem((ITERS, 2, TILES, RANK, LANES), F32),
        take=vmem((ITERS, 2, TILES, RANK, LANES), F32),
        give_ss=dma((ITERS, 2)),
        take_rs=dma((ITERS, 2)),
        part=vmem((ITERS, Z, HALF, LANES), F32),
        leaf=vmem((ITERS, len(LEAVES), HALF, LANES), F32),
        leaf_ss=dma((ITERS,)),
        leaf_rs=dma((ITERS, len(LEAVES))),
        relay=vmem((ITERS, len(RELAYS), HALF, LANES), BF16),
        final=vmem((ITERS, len(RELAYS), HALF, LANES), BF16),
        relay_ss=dma((ITERS,)),
        final_rs=dma((ITERS, len(RELAYS))),
        sub=vmem((2, Z, HALF, LANES), BF16),
        last=vmem((2, Z, HALF + CHUNK, LANES), BF16),
        sub_ss=dma((ITERS, 2)),
        sub_rs=dma((ITERS, Z)),
        proj=vmem((PAR, 2 * CHUNK, COLS), F32),
        proj_in=vmem((PAR - 1, 2 * CHUNK, COLS), F32),
        proj_ss=dma,
        proj_rs=dma,
        placed=vmem((LANES, COLS), F32),
        score=vmem((PAR, 8, LANES), F32),
        score_ss=dma,
        score_rs=dma,
    )
    names = ["grads", "start", "hook_out", "hook_in", "out"] + list(scratch)
    hbm = pl.BlockSpec(memory_space=pltpu.HBM)
    near = pl.BlockSpec(memory_space=pltpu.VMEM)

    def body(*refs):
        kernel(names, *refs)

    return pl.pallas_call(
        body,
        name="influence",
        out_shape=jax.ShapeDtypeStruct((QUERIES, ROWS), F32),
        in_specs=[hbm, hbm, hbm, hbm],
        out_specs=near,
        scratch_shapes=list(scratch.values()),
        compiler_params=pltpu.CompilerParams(
            collective_id=0, has_side_effects=True, vmem_limit_bytes=60 * 1024 * 1024
        ),
        cost_estimate=pl.CostEstimate(
            flops=8 * QUERIES * ROWS * FEATS * RANK, bytes_accessed=5_000_000, transcendentals=0
        ),
    )(query_grads, start_block.T, hooked_out, hooked_in)


def solution(mesh):
    placed = (P(None, "tok", "par"), P("par", "tok"), P("tok", "par"), P("tok", "par"))
    return jax.shard_map(
        on_device, mesh=mesh, in_specs=placed, out_specs=P(None, "tok"), check_vma=False
    )
```

```python
import types

import jax
import jax.numpy as jnp
from jax import lax
from jax.experimental import pallas as pl
from jax.experimental.pallas import tpu as pltpu
from jax.sharding import PartitionSpec as P

MESH = pl.DeviceIdType.MESH
F32, BF16 = jnp.float32, jnp.bfloat16
HIGH = lax.Precision.HIGHEST
RANK = 32
ITERS = 2
QUERIES = 4
COLS = QUERIES * RANK
LANES = 128
Z = 16
PAR = 16
ROWS = 256
FEATS = 1792
TILES = FEATS // LANES
OUTS = 512
PIECE = 512
PIECES = 4
CHUNK = ROWS // PAR
HALF = COLS // 2

TREE = {0: (1, -1), 3: (1, -1), -3: (1, -1), 6: (1, -1, 2), -6: (1, -1)}
RELAYS = (6, -6, 3, -3)
FAR = (8, 7, 9, 6, 10, 5, 11, 4, 12, 3, 13, 2, 14, 1, 15)
FAN = {0: (1, -1, 2, -2), 5: (1, -1, 2, -2, 3), -5: (1, -1, 2, -2)}
LEAVES = [(r, f) for r in (6, -6, 3, -3, 0) for f in TREE[r]]
SIDE = 4
ORDER = (10, 6, 14, 9, 11, 2, 8, 5, 15, 7, 13, 1, 3, 4, 12)


def nt(a, b, precision=None):
    return lax.dot_general(
        a, b, (((1,), (1,)), ((), ())), precision=precision, preferred_element_type=F32
    )


def remote(src, dst, send_sem, recv_sem, device):
    return pltpu.make_async_remote_copy(
        src_ref=src, dst_ref=dst, send_sem=send_sem, recv_sem=recv_sem,
        device_id=device, device_id_type=MESH,
    )


def drain(ref, sem):
    pltpu.make_async_copy(ref, ref, sem).wait()


def inverse_factor(gram):
    lane = lax.broadcasted_iota(jnp.int32, (RANK, COLS), 1)
    row = lax.broadcasted_iota(jnp.int32, (RANK, COLS), 0)
    first = lane - lane % RANK
    columns = [
        jnp.take_along_axis(gram, first + j, axis=1, mode="promise_in_bounds") for j in range(RANK)
    ]
    w = jnp.where(lane - first == row, 1.0, 0.0).astype(F32)
    for j in range(RANK):
        pivot = columns[j][j : j + 1, :]
        scale = lax.rsqrt(pivot)
        scale = scale * (1.5 - 0.5 * pivot * scale * scale)
        u = columns[j] * scale
        for k in range(j + 1, RANK):
            columns[k] = columns[k] - u * u[k : k + 1, :]
        row_w = w[j : j + 1, :] * scale
        w = jnp.where(row == j, row_w, jnp.where(row > j, w - u * row_w, w))
    return w


def block_diagonal(w):
    rows = lax.broadcasted_iota(jnp.int32, (COLS, COLS), 0)
    lanes = lax.broadcasted_iota(jnp.int32, (COLS, COLS), 1)
    return jnp.where(rows // RANK == lanes // RANK, jnp.concatenate([w] * QUERIES, axis=0), 0.0)


def kernel(names, *refs):
    m = types.SimpleNamespace(**dict(zip(names, refs)))
    tok, par = lax.axis_index("tok"), lax.axis_index("par")
    z, core = tok // 2, tok % 2

    def chip(offset):
        return (lax.rem(tok + 2 * offset + 2 * Z, 2 * Z), par)

    def at_z(offset):
        return lax.rem(z + offset + Z, Z)

    def peer(k):
        return lax.rem(par // SIDE + k // SIDE, SIDE) * SIDE + lax.rem(par + k, SIDE)

    sent = []
    sibling = (tok + 1 - 2 * core, par)

    loads = [
        pltpu.make_async_copy(m.grads.at[q], m.g.at[q], m.load_sem.at[q])
        for q in range(QUERIES)
    ] + [
        pltpu.make_async_copy(m.hook_out, m.ho, m.load_sem.at[QUERIES]),
        pltpu.make_async_copy(m.hook_in, m.hi, m.load_sem.at[QUERIES + 1]),
    ]
    load_start = pltpu.make_async_copy(m.start, m.begin, m.load_sem.at[QUERIES + 2])
    load_start.start()
    barrier = pltpu.get_barrier_semaphore()
    for k in FAR:
        pl.semaphore_signal(barrier, inc=1, device_id=chip(k), device_id_type=MESH)
    pl.semaphore_signal(barrier, inc=1, device_id=sibling, device_id_type=MESH)
    for k in ORDER:
        pl.semaphore_signal(barrier, inc=1, device_id=(tok, peer(k)), device_id_type=MESH)

    for load in loads:
        load.start()

    load_start.wait()
    start = m.begin[...].astype(F32)
    tail = jnp.concatenate(
        [start[:, 3 * PIECE :], jnp.zeros((start.shape[0], PIECES * PIECE - FEATS), F32)], axis=1
    )
    pieces = [start[:, k * PIECE : (k + 1) * PIECE] for k in range(PIECES - 1)] + [tail]
    m.s0[core, z] = jnp.concatenate(pieces, axis=0).astype(BF16)
    for it in range(ITERS):
        for k in range(TILES, Z):
            m.part[it, k] = jnp.zeros((HALF, LANES), F32)

    pl.semaphore_wait(barrier, Z - 1 + 1 + PAR - 1)

    def z_gather(buf, send_sem, recv_sem):
        own = buf.at[z]
        for r in (5, -5) + FAN[0]:
            remote(own, own, send_sem, recv_sem.at[r % Z], chip(r)).start()
        for r in (5, -5):
            block = buf.at[at_z(-r)]
            drain(block, recv_sem.at[r % Z])
            for f in FAN[r]:
                remote(block, block, send_sem, recv_sem.at[(r + f) % Z], chip(f)).start()
        relayed = [r % Z for r in (5, -5)]
        for k in range(1, Z):
            if k not in relayed:
                drain(buf.at[at_z(-k)], recv_sem.at[k])
        sent.append((buf.at[pl.ds(0, Z - 1)], send_sem))

    def par_scatter(src, dst, send_sem, recv_sem):
        for k in ORDER:
            remote(src.at[peer(k)], dst.at[k - 1], send_sem, recv_sem, (tok, peer(k))).start()
        sent.append((dst, send_sem))

    def par_gather(buf, send_sem, recv_sem):
        own = buf.at[par]
        for k in ORDER:
            remote(own, own, send_sem, recv_sem, (tok, peer(k))).start()
        sent.append((buf.at[pl.ds(0, PAR - 1)], send_sem))

    def swap(buf, send_sem, recv_sem):
        remote(buf.at[core], buf.at[core], send_sem, recv_sem, sibling).start()
        sent.append((buf.at[core], send_sem))

    z_gather(m.s0.at[core], m.s0_ss.at[0], m.s0_rs)
    swap(m.s0, m.s0_ss.at[1], m.s0_rs.at[0])
    for q in range(QUERIES):
        loads[q].wait()
    drain(m.s0.at[1 - core], m.s0_rs.at[0])
    even, odd = m.s0[0].astype(F32), m.s0[1].astype(F32)
    for k in range(PIECES):
        rows = slice(k * 4, k * 4 + 4)
        both = jnp.concatenate([even[:, rows, :], odd[:, rows, :]], axis=1)
        m.s0t[:, k * PIECE : (k + 1) * PIECE] = both.reshape(COLS, PIECE).astype(BF16)
    images = jnp.concatenate(
        [nt(m.g[q], m.s0t[q * RANK : (q + 1) * RANK, :FEATS]) for q in range(QUERIES)], axis=1
    )

    def tiles_of(buf, plane, first):
        return jnp.concatenate(
            [buf[plane, k, first : first + RANK, :] for k in range(TILES)], axis=1
        )

    for it in range(ITERS):
        m.img[it] = images.reshape(PAR, CHUNK, COLS)
        par_scatter(m.img.at[it], m.img_in.at[it], m.img_ss.at[it], m.img_rs.at[it])
        drain(m.img_in.at[it], m.img_rs.at[it])
        m.whole[it, par] = m.img[it, par] + jnp.sum(m.img_in[it], axis=0)
        par_gather(m.whole.at[it], m.whole_ss.at[it], m.whole_rs.at[it])
        drain(m.whole.at[it, pl.ds(0, PAR - 1)], m.whole_rs.at[it])

        if it == ITERS - 1:
            @pl.when(z == par)
            def _():
                for k in FAR:
                    remote(
                        m.whole.at[it, at_z(k)], m.brow, m.brow_ss, m.brow_rs, chip(k)
                    ).start()
                m.brow_own[...] = m.whole[it, z]

        turned = m.whole[it].reshape(ROWS, COLS).T
        gram = nt(turned, turned, HIGH)
        lane = lax.broadcasted_iota(jnp.int32, (RANK, COLS), 1)
        packed = jnp.zeros((RANK, COLS), F32)
        for q in range(QUERIES):
            packed = jnp.where(lane // RANK == q, gram[q * RANK : (q + 1) * RANK, :], packed)
        m.gram_out[it] = packed
        remote(
            m.gram_out.at[it], m.gram_in.at[it],
            m.gram_ss.at[it, 0], m.gram_rs.at[it, 0], sibling,
        ).start()
        sent.append((m.gram_out.at[it], m.gram_ss.at[it, 0]))

        high = turned.astype(BF16)
        low = (turned - high.astype(F32)).astype(BF16)
        for q in range(QUERIES):
            cut = slice(q * RANK, (q + 1) * RANK)
            m.split[q] = jnp.concatenate([high[cut], low[cut]], axis=0)

        def back(q):
            both = jnp.dot(m.split[q], m.g[q], preferred_element_type=F32)
            return both[:RANK] + both[RANK:]

        for i in range(2):
            terms = back(2 * (1 - core) + i)
            for k in range(TILES):
                m.give[it, i, k] = terms[:, k * LANES : (k + 1) * LANES]
            remote(
                m.give.at[it, i], m.take.at[it, i],
                m.give_ss.at[it, i], m.take_rs.at[it, i], sibling,
            ).start()
            sent.append((m.give.at[it, i], m.give_ss.at[it, i]))

        drain(m.gram_in.at[it], m.gram_rs.at[it, 0])
        m.gram_rows[it] = (packed + m.gram_in[it]).reshape(PAR, 2, COLS)
        mine = m.gram_rows.at[it, par]
        for k in FAR:
            remote(
                mine, m.gram_z.at[it, k - 1], m.gram_ss.at[it, 1], m.gram_rs.at[it, 1], chip(k)
            ).start()
        sent.append((m.gram_z.at[it], m.gram_ss.at[it, 1]))

        for i in range(2):
            terms = back(2 * core + i)
            drain(m.take.at[it, i], m.take_rs.at[it, i])
            for k in range(TILES):
                both = terms[:, k * LANES : (k + 1) * LANES] + m.take[it, i, k]
                m.part[it, k, i * RANK : (i + 1) * RANK, :] = both

        part = m.part.at[it]
        for slot, (r, f) in enumerate(LEAVES):
            remote(
                part.at[at_z(-r - f)], m.leaf.at[it, slot],
                m.leaf_ss.at[it], m.leaf_rs.at[it, slot], chip(-f),
            ).start()
        sent.append((m.leaf.at[it], m.leaf_ss.at[it]))

        drain(m.gram_z.at[it], m.gram_rs.at[it, 1])
        m.gram_all[it, par] = m.gram_rows[it, par] + jnp.sum(m.gram_z[it], axis=0)
        par_gather(m.gram_all.at[it], m.gram_ss.at[it, 2], m.gram_rs.at[it, 2])

        for n, r in enumerate(RELAYS):
            total = m.part[it, at_z(-r)]
            for slot, (rr, f) in enumerate(LEAVES):
                if rr == r:
                    drain(m.leaf.at[it, slot], m.leaf_rs.at[it, slot])
                    total = total + m.leaf[it, slot]
            m.relay[it, n] = total.astype(BF16)
            remote(
                m.relay.at[it, n], m.final.at[it, n],
                m.relay_ss.at[it], m.final_rs.at[it, n], chip(-r),
            ).start()
        sent.append((m.relay.at[it], m.relay_ss.at[it]))

        drain(m.gram_all.at[it, pl.ds(0, PAR - 1)], m.gram_rs.at[it, 2])
        full = m.gram_all[it].reshape(RANK, COLS)
        inverse = block_diagonal(inverse_factor(full))
        inverse_mine = jnp.where(
            core == 0, inverse[:HALF, :HALF], inverse[HALF:, HALF:]
        )

        total = m.part[it, z]
        for slot, (r, f) in enumerate(LEAVES):
            if r == 0:
                drain(m.leaf.at[it, slot], m.leaf_rs.at[it, slot])
                total = total + m.leaf[it, slot]
        for n in range(len(RELAYS)):
            drain(m.final.at[it, n], m.final_rs.at[it, n])
            total = total + m.final[it, n].astype(F32)
        turned_back = jnp.dot(inverse_mine, total, precision=HIGH, preferred_element_type=F32)
        sub = m.sub if it < ITERS - 1 else m.last
        sub[core, z, :HALF, :] = turned_back.astype(BF16)
        if it == ITERS - 1:
            @pl.when(z != par)
            def _():
                drain(m.brow, m.brow_rs)
                m.brow_own[...] = m.brow[...]
            sub[core, z, HALF:, :] = nt(m.brow_own[...], inverse, HIGH).astype(BF16)

        z_gather(sub.at[core], m.sub_ss.at[it, 0], m.sub_rs.at[it])
        swap(sub, m.sub_ss.at[it, 1], m.sub_rs.at[it, 0])
        if it < ITERS - 1:
            def pair(plane):
                return jnp.concatenate(
                    [nt(m.g[2 * plane + i], tiles_of(sub, plane, i * RANK)) for i in range(2)], axis=1
                )

            ours = pair(core)
            drain(sub.at[1 - core], m.sub_rs.at[it, 0])
            theirs = pair(1 - core)
            images = jnp.where(
                core == 0,
                jnp.concatenate([ours, theirs], axis=1),
                jnp.concatenate([theirs, ours], axis=1),
            )
        else:
            drain(sub.at[1 - core], m.sub_rs.at[it, 0])

    loads[QUERIES].wait()
    loads[QUERIES + 1].wait()
    last = m.last
    basis = jnp.concatenate(
        [last[plane, :, HALF:, :].reshape(ROWS, COLS) for plane in range(2)], axis=0
    )
    out_proj = jnp.dot(m.ho[...], basis, preferred_element_type=F32)
    m.proj[0] = out_proj.reshape(PAR, CHUNK, COLS)
    par_scatter(m.proj.at[0], m.proj_in.at[0], m.proj_ss.at[0], m.proj_rs.at[0])
    subspace = jnp.concatenate(
        [tiles_of(last, q // 2, (q % 2) * RANK) for q in range(QUERIES)], axis=0
    )
    in_proj = nt(m.hi[...], subspace)
    m.proj[1] = in_proj.reshape(PAR, CHUNK, COLS)
    par_scatter(m.proj.at[1], m.proj_in.at[1], m.proj_ss.at[1], m.proj_rs.at[1])
    lane8 = lax.broadcasted_iota(jnp.int32, (8, COLS), 1)
    row8 = lax.broadcasted_iota(jnp.int32, (8, COLS), 0)
    pick = jnp.where(lane8 // RANK == row8, 1.0, 0.0).astype(F32)
    m.placed[...] = jnp.zeros((LANES, COLS), F32)
    sums = []
    for n in range(2):
        drain(m.proj_in.at[n], m.proj_rs.at[n])
        sums.append(m.proj[n, par] + jnp.sum(m.proj_in[n], axis=0))
    m.placed[pl.ds(pl.multiple_of((par % 8) * CHUNK, CHUNK), CHUNK), :] = (
        sums[0] * sums[1]
    )
    m.score[par] = nt(pick, m.placed[...], HIGH)
    par_gather(m.score, m.score_ss, m.score_rs)
    drain(m.score.at[pl.ds(0, PAR - 1)], m.score_rs)
    for h in range(2):
        m.out[:, h * LANES : (h + 1) * LANES] = jnp.sum(
            m.score[h * 8 : h * 8 + 8], axis=0
        )[:QUERIES]

    for ref, sem in sent:
        drain(ref, sem)

    @pl.when(z == par)
    def _():
        drain(m.whole.at[ITERS - 1, pl.ds(0, Z - 1)], m.brow_ss)


def on_device(query_grads, start_block, hooked_out, hooked_in):
    vmem, dma = pltpu.VMEM, pltpu.SemaphoreType.DMA
    scratch = dict(
        g=vmem((QUERIES, ROWS, FEATS), BF16),
        ho=vmem((ROWS, OUTS), BF16),
        hi=vmem((ROWS, FEATS), BF16),
        begin=vmem((QUERIES, FEATS), BF16),
        load_sem=dma((QUERIES + 3,)),
        s0=vmem((2, Z, 4 * PIECES, PIECE), BF16),
        s0_ss=dma((2,)),
        s0_rs=dma((Z,)),
        s0t=vmem((COLS, PIECES * PIECE), BF16),
        img=vmem((ITERS, PAR, CHUNK, COLS), F32),
        img_in=vmem((ITERS, PAR - 1, CHUNK, COLS), F32),
        img_ss=dma((ITERS,)),
        img_rs=dma((ITERS,)),
        whole=vmem((ITERS, PAR, CHUNK, COLS), F32),
        whole_ss=dma((ITERS,)),
        whole_rs=dma((ITERS,)),
        brow=vmem((CHUNK, COLS), F32),
        brow_own=vmem((CHUNK, COLS), F32),
        brow_ss=dma,
        brow_rs=dma,
        gram_out=vmem((ITERS, RANK, COLS), F32),
        gram_in=vmem((ITERS, RANK, COLS), F32),
        gram_rows=vmem((ITERS, PAR, 2, COLS), F32),
        gram_z=vmem((ITERS, Z - 1, 2, COLS), F32),
        gram_all=vmem((ITERS, PAR, 2, COLS), F32),
        gram_ss=dma((ITERS, 3)),
        gram_rs=dma((ITERS, 3)),
        split=vmem((QUERIES, 2 * RANK, ROWS), BF16),
        give=vmem((ITERS, 2, TILES, RANK, LANES), F32),
        take=vmem((ITERS, 2, TILES, RANK, LANES), F32),
        give_ss=dma((ITERS, 2)),
        take_rs=dma((ITERS, 2)),
        part=vmem((ITERS, Z, HALF, LANES), F32),
        leaf=vmem((ITERS, len(LEAVES), HALF, LANES), F32),
        leaf_ss=dma((ITERS,)),
        leaf_rs=dma((ITERS, len(LEAVES))),
        relay=vmem((ITERS, len(RELAYS), HALF, LANES), BF16),
        final=vmem((ITERS, len(RELAYS), HALF, LANES), BF16),
        relay_ss=dma((ITERS,)),
        final_rs=dma((ITERS, len(RELAYS))),
        sub=vmem((2, Z, HALF, LANES), BF16),
        last=vmem((2, Z, HALF + CHUNK, LANES), BF16),
        sub_ss=dma((ITERS, 2)),
        sub_rs=dma((ITERS, Z)),
        proj=vmem((2, PAR, CHUNK, COLS), F32),
        proj_in=vmem((2, PAR - 1, CHUNK, COLS), F32),
        proj_ss=dma((2,)),
        proj_rs=dma((2,)),
        placed=vmem((LANES, COLS), F32),
        score=vmem((PAR, 8, LANES), F32),
        score_ss=dma,
        score_rs=dma,
    )
    names = ["grads", "start", "hook_out", "hook_in", "out"] + list(scratch)
    hbm = pl.BlockSpec(memory_space=pltpu.HBM)
    near = pl.BlockSpec(memory_space=pltpu.VMEM)

    def body(*refs):
        kernel(names, *refs)

    return pl.pallas_call(
        body,
        name="influence",
        out_shape=jax.ShapeDtypeStruct((QUERIES, ROWS), F32),
        in_specs=[hbm, hbm, hbm, hbm],
        out_specs=near,
        scratch_shapes=list(scratch.values()),
        compiler_params=pltpu.CompilerParams(
            collective_id=0, has_side_effects=True, vmem_limit_bytes=60 * 1024 * 1024
        ),
        cost_estimate=pl.CostEstimate(
            flops=8 * QUERIES * ROWS * FEATS * RANK, bytes_accessed=5_000_000, transcendentals=0
        ),
    )(query_grads, start_block.T, hooked_out, hooked_in)


def solution(mesh):
    placed = (P(None, "tok", "par"), P("par", "tok"), P("tok", "par"), P("tok", "par"))
    return jax.shard_map(
        on_device, mesh=mesh, in_specs=placed, out_specs=P(None, "tok"), check_vma=False
    )
```
